32 devices in a mesh: dp: 4 (over y, core), tensor: 8 (over z, x).
Axes of the slice: x: 2, y: 2, z: 4, core: 2. Of those that a mesh axis runs over, the one named last changes fastest.
Arguments:
- tokens: bfloat16 [1024, 24, 1152], P('tensor', 'dp'), may hold values from -6 to 6
- condition: bfloat16 [24, 1152], P('dp'), may hold values from -6 to 6
- counts: int32 [4], P('dp'), may hold values from 1 to 6, as said below
- ada_weight: bfloat16 [1152, 6912], P(None, 'tensor'), may hold values from -0.1875 to 0.1875
- ada_bias: bfloat16 [6912], P('tensor'), may hold values from -3 to 3
- qkv_weight: bfloat16 [1152, 3, 1152], P(None, None, 'tensor'), may hold values from -0.1875 to 0.1875
- qkv_bias: bfloat16 [2, 1152], P(None, 'tensor'), may hold values from -3 to 3
- out_weight: bfloat16 [1152, 1152], P('tensor'), may hold values from -3 to 3
- out_bias: bfloat16 [1152], replicated, may hold values from -3 to 3
- fc1_weight: bfloat16 [1152, 4608], P(None, 'tensor'), may hold values from -0.1875 to 0.1875
- fc1_bias: bfloat16 [4608], P('tensor'), may hold values from -3 to 3
- fc2_weight: bfloat16 [4608, 1152], P('tensor'), may hold values from -0.25 to 0.25
- fc2_bias: bfloat16 [1152], replicated, may hold values from -3 to 3
- out_grad: bfloat16 [1024, 24, 1152], P('tensor', 'dp'), may hold values from -6 to 6
Outputs:
- output: bfloat16 [1024, 24, 1152], P('tensor', 'dp')
- tokens_grad: float32 [1024, 24, 1152], P('tensor', 'dp')
- condition_grad: float32 [24, 1152], P('dp')
- ada_weight_grad: float32 [1152, 6912], P(None, 'tensor')
- ada_bias_grad: float32 [6912], P('tensor')
- qkv_weight_grad: float32 [1152, 3, 1152], P(None, None, 'tensor')
- qkv_bias_grad: float32 [2, 1152], P(None, 'tensor')
- out_weight_grad: float32 [1152, 1152], P('tensor')
- out_bias_grad: float32 [1152], replicated
- fc1_weight_grad: float32 [1152, 4608], P(None, 'tensor')
- fc1_bias_grad: float32 [4608], P('tensor')
- fc2_weight_grad: float32 [4608, 1152], P('tensor')
- fc2_bias_grad: float32 [1152], replicated
The draws below stay inside these ranges and needn't reach their ends.
Inputs may be any that keep to these rules, and one draw needn't show every extreme that they name: `counts`: slots of a dp index below its count hold latents, the rest are empty; some dp index holds 6 latents and some holds 1.
All inputs are finite; a program needn't handle non-finite values.
Results may differ from the reference program's by a relative error of at most 0.01145.
The reference program's roundings to bfloat16 on the way count: a program that leaves them out, or rounds other values in their place, can miss the bound.
Values may be sent and summed in bfloat16 or wider, within the bound.
No kernel may reach another device: no remote copies, remote signals or barrier semaphores. Data moves between devices by JAX's collectives and lax.ppermute only.
A program may use at most 320 MiB of HBM per device.

```python
import jax
import jax.numpy as jnp
from jax import lax

D = 1152
HEADS = 16
HDIM = 72
FF = 4608
TOK = 1024
CAP = 6
SLOTS = 24
N_DP = 4


def draw_counts(key, part):
    key = jax.random.fold_in(key, 7)
    first_key, second_key = jax.random.split(key, 2)
    number = SLOTS // CAP
    values = jax.random.randint(first_key, (number,), 1, CAP + 1)
    shuffled = jax.random.permutation(second_key, number)
    values = values.at[shuffled[0]].set(CAP)
    values = values.at[shuffled[1]].set(1)
    return values.astype(jnp.int32)


def strengthened(drawn, key, source, target, blocks, factor):
    def block_of(axis_at):
        return (jnp.arange(drawn.shape[axis_at]) // (drawn.shape[axis_at] // blocks)).reshape((-1,) + (1,) * (drawn.ndim - 1 - axis_at))

    one_side = jax.random.permutation(key, blocks)[block_of(target)]
    far = (block_of(target) + blocks // 2) % blocks
    return jnp.where((block_of(source) == one_side) | (block_of(source) == far), factor * drawn, drawn)


def block_levels(own_key, shape, shards, least, top_value):
    factor_of, own = 1.0, jax.random.fold_in(own_key, 6)
    for axis_at, parts in shards:
        heights = jnp.exp(jax.random.uniform(jax.random.fold_in(own, axis_at), (parts,), jnp.float32, least / len(shards), top_value / len(shards)))
        factor_of = factor_of * jnp.repeat(heights, shape[axis_at] // parts).reshape([-1 if axis == axis_at else 1 for axis in range(len(shape))])
    return factor_of


def gaussian(rng, extent, spread, bound, cuts=(), dtype=jnp.bfloat16):
    entries = spread * jax.random.normal(rng, extent, jnp.float32)
    if cuts:
        entries = entries * block_levels(rng, extent, cuts, -0.22, 0.18)
    return jnp.clip(entries, -bound, bound).astype(dtype)


def noise_with(rng, shape, spread, bound, cuts, heavy, dtype=jnp.bfloat16):
    values = spread * jax.random.normal(rng, shape, jnp.float32)
    if cuts:
        values = values * block_levels(rng, shape, cuts, -0.22, 0.18)
    return jnp.clip(strengthened(values, jax.random.fold_in(rng, 3), *heavy), -bound, bound).astype(dtype)


def setup_inputs(seed: int = 0) -> dict:
    splits = jax.random.split(jax.random.key(seed), 15)
    tokens = gaussian(splits[0], (TOK, SLOTS, D), 1.0, 6.0, ((0, 8), (1, 4)))
    condition = gaussian(splits[1], (SLOTS, D), 1.0, 6.0, ((0, 4),))
    counts = draw_counts(jax.random.fold_in(splits[14], 71), 0)
    ada_weight = gaussian(splits[3], (D, 6 * D), D ** -0.5, 0.1875, ((1, 8),))
    ada_bias = gaussian(splits[4], (6 * D,), 0.5, 3.0, ((0, 8),))
    qkv_weight = gaussian(splits[5], (D, 3, D), D ** -0.5, 0.1875, ((2, 8),))
    qkv_bias = gaussian(splits[6], (2, D), 0.5, 3.0, ((1, 8),))
    out_weight = gaussian(splits[7], (D, D), (max(D // 256, 1)) ** -0.5, 3.0, ((0, 8),))
    out_bias = gaussian(splits[8], (D,), 0.5, 3.0)
    fc1_weight = gaussian(splits[9], (D, FF), D ** -0.5, 0.1875, ((1, 8),))
    fc1_bias = gaussian(splits[10], (FF,), 0.5, 3.0, ((0, 8),))
    fc2_weight = noise_with(splits[11], (FF, D), (max(FF // 4, 1)) ** -0.5, 0.25, ((0, 8),), (0, 1, 8, 2.0))
    fc2_bias = gaussian(splits[12], (D,), 0.5, 3.0)
    out_grad = gaussian(splits[13], (TOK, SLOTS, D), 1.0, 6.0, ((0, 8), (1, 4)))
    return {"tokens": tokens, "condition": condition, "counts": counts, "ada_weight": ada_weight, "ada_bias": ada_bias, "qkv_weight": qkv_weight, "qkv_bias": qkv_bias, "out_weight": out_weight, "out_bias": out_bias, "fc1_weight": fc1_weight, "fc1_bias": fc1_bias, "fc2_weight": fc2_weight, "fc2_bias": fc2_bias, "out_grad": out_grad}


@jax.custom_vjp
def low(v):
    return lax.optimization_barrier(v.astype(jnp.bfloat16)).astype(jnp.float32)

@jax.custom_vjp
def low_back(v):
    return v

def low_keep(v):
    return (low(v), None)

def low_pass(kept, grad):
    return (grad,)

def back_keep(v):
    return (v, None)

def back_low(kept, grad):
    return (low(grad),)
low.defvjp(low_keep, low_pass)
low_back.defvjp(back_keep, back_low)

def exact(form, left, right):
    return jnp.einsum(form, left, right, precision=lax.Precision.HIGHEST)

def layer_norm(values):
    average = lax.optimization_barrier(jnp.mean(values, axis=-1, keepdims=True))
    centred = values - average
    variance = lax.optimization_barrier(jnp.mean(centred * centred, axis=-1, keepdims=True))
    return centred * lax.rsqrt(variance + 1e-06)

def attend_one(pieces):
    query_rows, key_rows, value_rows = pieces
    scores = low_back(exact('qhe,khe->hqk', query_rows, key_rows) * query_rows.shape[-1] ** (-0.5))
    row_peak = lax.optimization_barrier(jnp.max(scores, axis=-1, keepdims=True))
    raised = jnp.exp(scores - row_peak)
    soft_low = low(raised / lax.optimization_barrier(jnp.sum(raised, axis=-1, keepdims=True)))
    return exact('hqk,khe->qhe', soft_low, value_rows)

def forward(tokens, condition, ada_weight, ada_bias, qkv_weight, qkv_bias, out_weight, out_bias, fc1_weight, fc1_bias, fc2_weight, fc2_bias):
    seq_len, slot_count, model_width = tokens.shape
    activated = low(jax.nn.silu(condition))
    modulation = low_back(exact('sd,df->sf', activated, ada_weight) + ada_bias)
    shift_attn, scale_attn, gate_attn, shift_mlp, scale_mlp, gate_mlp = [modulation[None, :, column * model_width:(column + 1) * model_width] for column in range(6)]
    normed_attn = layer_norm(tokens)
    hidden_attn = low(normed_attn * (1.0 + scale_attn) + shift_attn)
    bias_full = jnp.stack([qkv_bias[0], jnp.zeros_like(qkv_bias[0]), qkv_bias[1]])
    projected = low_back(low(exact('tsd,dcf->tscf', hidden_attn, qkv_weight) + bias_full))
    head_shape = (seq_len, slot_count, HEADS, HDIM)
    query_rows = jnp.moveaxis(projected[:, :, 0].reshape(head_shape), 1, 0)
    key_rows = jnp.moveaxis(projected[:, :, 1].reshape(head_shape), 1, 0)
    value_rows = jnp.moveaxis(projected[:, :, 2].reshape(head_shape), 1, 0)
    attended = lax.map(jax.checkpoint(attend_one), (query_rows, key_rows, value_rows))
    attended = jnp.moveaxis(attended, 0, 1).reshape(seq_len, slot_count, model_width)
    attended = low_back(low(attended))
    attn_branch = low_back(exact('tsf,fd->tsd', attended, out_weight) + out_bias)
    mixed = tokens + gate_attn * attn_branch
    normed_mlp = layer_norm(mixed)
    hidden_mlp = low(normed_mlp * (1.0 + scale_mlp) + shift_mlp)
    pre_act = low_back(exact('tsd,df->tsf', hidden_mlp, fc1_weight) + fc1_bias)
    activ = low(jax.nn.gelu(pre_act, approximate=True))
    mlp_branch = low_back(exact('tsf,fd->tsd', activ, fc2_weight) + fc2_bias)
    return mixed + gate_mlp * mlp_branch

def reference(tokens, condition, counts, ada_weight, ada_bias, qkv_weight, qkv_bias, out_weight, out_bias, fc1_weight, fc1_bias, fc2_weight, fc2_bias, out_grad):
    weights = tuple((item.astype(jnp.float32) for item in (ada_weight, ada_bias, qkv_weight, qkv_bias, out_weight, out_bias, fc1_weight, fc1_bias, fc2_weight, fc2_bias)))
    live_mask = (jnp.arange(CAP)[None, :] < counts[:, None]).astype(jnp.float32)
    grouped_tokens = jnp.moveaxis(tokens.astype(jnp.float32).reshape(TOK, N_DP, CAP, D), 1, 0)
    grouped_grad = jnp.moveaxis(out_grad.astype(jnp.float32).reshape(TOK, N_DP, CAP, D), 1, 0)
    grouped_cond = condition.astype(jnp.float32).reshape(N_DP, CAP, D)

    def one_group(totals, pieces):
        group_tokens, group_cond, group_grad, group_live = pieces
        result, pullback = jax.vjp(forward, group_tokens, group_cond, *weights)
        gradients = pullback(group_grad * group_live[None, :, None])
        totals = tuple((first + second for first, second in zip(totals, gradients[2:])))
        return (totals, (result * group_live[None, :, None], gradients[0], gradients[1]))
    zeros_start = tuple((jnp.zeros_like(item) for item in weights))
    totals, (results, token_grads, cond_grads) = lax.scan(one_group, zeros_start, (grouped_tokens, grouped_cond, grouped_grad, live_mask))
    output = jnp.moveaxis(results, 0, 1).reshape(TOK, SLOTS, D).astype(jnp.bfloat16)
    tokens_grad = jnp.moveaxis(token_grads, 0, 1).reshape(TOK, SLOTS, D)
    condition_grad = cond_grads.reshape(SLOTS, D)
    return (output, tokens_grad, condition_grad, totals[0], totals[1], totals[2], totals[3], totals[4], totals[5], totals[6], totals[7], totals[8], totals[9])
```

```python
import functools

import jax
import jax.numpy as jnp
from jax import lax
from jax.experimental import pallas as pl
from jax.experimental.pallas import tpu as pltpu
from jax.sharding import PartitionSpec as P

HDIM = 72
LOW = jnp.bfloat16
FULL = jnp.float32
LAST = (((1,), (1,)), ((), ()))
FIRST = (((0,), (0,)), ((), ()))
PLAIN = (((1,), (0,)), ((), ()))
ROWS = 256


def dot(left, right, dims=PLAIN):
    return lax.dot_general(left, right, dims, preferred_element_type=FULL)


def layer_norm(values):
    average = jnp.mean(values, axis=-1, keepdims=True)
    centred = values - average
    variance = jnp.mean(centred * centred, axis=-1, keepdims=True)
    scale = lax.rsqrt(variance + 1e-06)
    return centred * scale, scale


def norm_back(normed, scale, grad):
    first = jnp.mean(grad, axis=-1, keepdims=True)
    second = jnp.mean(grad * normed, axis=-1, keepdims=True)
    return (grad - first - normed * second) * scale


def gelu_tanh(values):
    return jax.nn.gelu(values, approximate=True)


def soft_rows(query_block, keys):
    scores = dot(query_block, keys, LAST)
    peak = jnp.max(scores, axis=-1, keepdims=True)
    raised = jnp.exp((scores - peak) * (HDIM**-0.5))
    return raised * (1.0 / jnp.sum(raised, axis=-1, keepdims=True))


def column(head, part):
    return (head * 3 + part) * HDIM


def attend_kernel(heads, base, projected, attended, queries, keys, values, results):
    seq = projected.shape[0]
    block = min(ROWS, seq)
    for head in range(heads):
        for part, held in enumerate((queries, keys, values)):
            at = base + column(head, part)
            held[head] = projected[:, at : at + HDIM]

    def one_head(head, carry):
        key_rows, value_rows = keys[head], values[head]
        for start in range(0, seq, block):
            soft = soft_rows(queries[head, start : start + block], key_rows)
            results[head, start : start + block] = dot(soft.astype(LOW), value_rows).astype(LOW)
        return carry

    lax.fori_loop(0, heads, one_head, 0)
    for head in range(heads):
        attended[:, head * HDIM : (head + 1) * HDIM] = results[head]


def attend(projected, heads, chunk):
    seq = projected.shape[0]
    held = pltpu.VMEM((heads, seq, HDIM), LOW)
    return pl.pallas_call(
        functools.partial(attend_kernel, heads, chunk * column(heads, 0)),
        out_shape=jax.ShapeDtypeStruct((seq, heads * HDIM), LOW),
        in_specs=[pl.BlockSpec(memory_space=pltpu.VMEM)],
        out_specs=pl.BlockSpec(memory_space=pltpu.VMEM),
        scratch_shapes=[held, held, held, held],
        compiler_params=pltpu.CompilerParams(vmem_limit_bytes=48 * 1024 * 1024),
        cost_estimate=pl.CostEstimate(
            flops=heads * seq * seq * 2048,
            bytes_accessed=8 * heads * HDIM * seq,
            transcendentals=heads * seq * seq,
        ),
    )(projected)


def attend_back_kernel(
    heads, base, projected, attended_grad, projected_grad, queries, keys, values, grads
):
    seq = projected.shape[0]
    block = min(ROWS, seq)
    score_scale = HDIM**-0.5
    first = base // 3
    for head in range(heads):
        for part, held in enumerate((queries, keys, values)):
            at = base + column(head, part)
            held[head] = projected[:, at : at + HDIM]
        at = first + head * HDIM
        grads[head] = attended_grad[:, at : at + HDIM]

    def one_head(head, carry):
        key_rows, value_rows = keys[head], values[head]
        key_total = value_total = None
        for start in range(0, seq, block):
            query_block = queries[head, start : start + block]
            grad_block = grads[head, start : start + block]
            soft = soft_rows(query_block, key_rows)
            soft_grad = dot(grad_block, value_rows, LAST)
            row_dot = jnp.sum(soft * soft_grad, axis=-1, keepdims=True)
            score_grad = (soft * (soft_grad - row_dot)).astype(LOW)
            queries[head, start : start + block] = (
                dot(score_grad, key_rows) * score_scale
            ).astype(LOW)
            key_part = dot(query_block, score_grad, FIRST)
            value_part = dot(grad_block, soft.astype(LOW), FIRST)
            key_total = key_part if key_total is None else key_total + key_part
            value_total = value_part if value_total is None else value_total + value_part
        keys[head] = (key_total * score_scale).T.astype(LOW)
        values[head] = value_total.T.astype(LOW)
        return carry

    lax.fori_loop(0, heads, one_head, 0)
    for head in range(heads):
        for part, held in enumerate((queries, keys, values)):
            at = column(head, part)
            projected_grad[:, at : at + HDIM] = held[head]


def attend_back(projected, attended_grad, heads, chunk):
    seq = projected.shape[0]
    held = pltpu.VMEM((heads, seq, HDIM), LOW)
    whole = pl.BlockSpec(memory_space=pltpu.VMEM)
    return pl.pallas_call(
        functools.partial(attend_back_kernel, heads, chunk * column(heads, 0)),
        out_shape=jax.ShapeDtypeStruct((seq, column(heads, 0)), LOW),
        in_specs=[whole, whole],
        out_specs=whole,
        scratch_shapes=[held, held, held, held],
        compiler_params=pltpu.CompilerParams(vmem_limit_bytes=48 * 1024 * 1024),
        cost_estimate=pl.CostEstimate(
            flops=heads * seq * seq * 4096,
            bytes_accessed=14 * heads * HDIM * seq,
            transcendentals=heads * seq * seq,
        ),
    )(projected, attended_grad)


def low(values):
    return lax.optimization_barrier(values.astype(LOW))


def add(*terms):
    total = terms[0].astype(FULL)
    for term in terms[1:]:
        total = total + term.astype(FULL)
    return total


def partner(values, axis, bit):
    return lax.ppermute(values, axis, [(i, i ^ bit) for i in range(lax.axis_size(axis))])


def bits_of(axis, start=1):
    found, bit = [], start
    while bit < lax.axis_size(axis):
        found.append(bit)
        bit *= 2
    return found


def order_by(flag, one, two, axis):
    return jnp.concatenate([jnp.where(flag, two, one), jnp.where(flag, one, two)], axis=axis)


def pair_sum(values, axis, start=1):
    for bit in bits_of(axis, start):
        values = values + partner(values, axis, bit)
    return values


def pair_gather(values, axis):
    here = lax.axis_index(axis)
    held = values[None]
    for bit in bits_of(axis):
        held = order_by((here & bit) != 0, held, partner(held, axis, bit), 0)
    return held


def after(value, *others):
    return lax.optimization_barrier((value, *others))[0]


def gather_weight(shard):
    share = shard.shape[0] // lax.axis_size("dp")
    mine = lax.dynamic_slice_in_dim(shard, lax.axis_index("dp") * share, share, 0)
    return lax.all_gather(mine, ("tensor", "dp"), axis=0, tiled=True)


def reduce_weight(grad):
    mine = lax.psum_scatter(grad, ("tensor", "dp"), scatter_dimension=0, tiled=True)
    return pair_gather(mine, "dp").reshape(-1, grad.shape[1])


def slot_start(slots):
    return (lax.axis_size("tensor") - slots) // 2


def to_slots(pieces):
    slots, rows, width = pieces.shape
    groups, here = lax.axis_size("tensor"), lax.axis_index("tensor")
    start = slot_start(slots)
    parts = []
    for step in range(groups):
        slot = jnp.clip(lax.rem(here + step, groups) - start, 0, slots - 1)
        piece = lax.dynamic_index_in_dim(pieces, slot, 0, False)
        if step:
            pairs = [(i, (i + step) % groups) for i in range(groups)]
            pairs = [pair for pair in pairs if start <= pair[1] < start + slots]
            piece = lax.ppermute(piece, "tensor", pairs)
        parts.append(piece)
    return jnp.concatenate(parts, axis=0)


def from_slots(values, slots):
    groups, here = lax.axis_size("tensor"), lax.axis_index("tensor")
    start = slot_start(slots)
    rows = values.shape[0] // groups
    parts = []
    for step in range(groups):
        piece = values[step * rows : (step + 1) * rows]
        if step:
            pairs = [((i + step) % groups, i) for i in range(groups)]
            pairs = [pair for pair in pairs if start <= pair[0] < start + slots]
            piece = lax.ppermute(piece, "tensor", pairs)
        parts.append(piece)
    twice = jnp.stack(parts + parts, axis=0)
    return lax.dynamic_slice_in_dim(twice, lax.rem(groups + start - here, groups), slots, 0)


def on_device(
    tokens,
    condition,
    counts,
    ada_weight,
    ada_bias,
    qkv_weight,
    qkv_bias,
    out_weight,
    out_bias,
    fc1_weight,
    fc1_bias,
    fc2_weight,
    fc2_bias,
    out_grad,
):
    local_rows, slots, width = tokens.shape
    groups, here = lax.axis_size("tensor"), lax.axis_index("tensor")
    assert slots <= groups
    seq = local_rows * groups
    local_width = qkv_weight.shape[2]
    local = local_width // HDIM
    three = 3 * HDIM
    unit = 4 * HDIM
    start = slot_start(slots)
    hidden_local = fc1_weight.shape[1]
    live = ((here >= start) & (here - start < counts[0])).astype(FULL)

    qkv_rows = jnp.transpose(qkv_weight, (1, 2, 0)).reshape(3, local, HDIM, width)
    out_rows = out_weight.reshape(1, local, HDIM, width)
    first = jnp.transpose(jnp.concatenate([qkv_rows, out_rows]), (1, 0, 2, 3))
    first = gather_weight(first.reshape(local * unit, width)).reshape(groups, local, unit, width)
    fc1_full = gather_weight(fc1_weight.T)
    fc2_full = gather_weight(fc2_weight)
    first = jnp.transpose(first, (1, 0, 2, 3))
    qkv_full = first[:, :, :three].reshape(-1, width)
    out_full = first[:, :, three:].reshape(-1, width)

    silu_value, silu_back = jax.vjp(jax.nn.silu, condition.astype(FULL))
    activated = silu_value.astype(LOW)
    mod_local = dot(activated, ada_weight) + ada_bias.astype(FULL)
    mod_width = mod_local.shape[1]
    qkv_three = jnp.stack([qkv_bias[0], jnp.zeros_like(qkv_bias[0]), qkv_bias[1]])
    qkv_three = jnp.transpose(qkv_three.reshape(3, local, HDIM), (1, 0, 2)).reshape(-1).astype(FULL)
    small = jnp.concatenate([mod_local.reshape(-1), qkv_three, fc1_bias.astype(FULL)])
    small = pair_gather(small, "tensor")
    slot = jnp.clip(here - start, 0, slots - 1)
    modulation = small[:, : slots * mod_width].reshape(groups, slots, mod_width)
    modulation = lax.dynamic_index_in_dim(modulation, slot, 1, False).reshape(6, 1, width)
    shift_attn, scale_attn, gate_attn, shift_mlp, scale_mlp, gate_mlp = modulation
    qkv_bias_full = small[:, slots * mod_width : slots * mod_width + local * three]
    qkv_bias_full = jnp.transpose(qkv_bias_full.reshape(groups, local, three), (1, 0, 2)).reshape(-1)
    fc1_bias_full = small[:, slots * mod_width + local * three :].reshape(-1)

    inputs = to_slots(jnp.transpose(tokens, (1, 0, 2))).astype(FULL)
    normed_attn, attn_scale = layer_norm(inputs)
    hidden_attn = (normed_attn * (1.0 + scale_attn) + shift_attn).astype(LOW)
    projected = (dot(hidden_attn, qkv_full, LAST) + qkv_bias_full).astype(LOW)
    attended = [attend(projected, groups, chunk) for chunk in range(local)]
    attended = jnp.concatenate(attended, axis=1)
    attn_branch = dot(attended, out_full) + out_bias.astype(FULL)
    mixed = inputs + gate_attn * attn_branch
    normed_mlp, mlp_scale = layer_norm(mixed)
    hidden_mlp = (normed_mlp * (1.0 + scale_mlp) + shift_mlp).astype(LOW)
    pre_act = dot(hidden_mlp, fc1_full, LAST) + fc1_bias_full
    activ_value, gelu_back = jax.vjp(gelu_tanh, pre_act)
    activ = activ_value.astype(LOW)
    mlp_branch = dot(activ, fc2_full) + fc2_bias.astype(FULL)
    output = (live * (mixed + gate_mlp * mlp_branch)).astype(LOW)
    output = jnp.transpose(from_slots(output, slots), (1, 0, 2))

    out_grad, _ = lax.optimization_barrier((out_grad, projected))
    upstream = live * to_slots(jnp.transpose(out_grad, (1, 0, 2))).astype(FULL)
    branch_grad = (gate_mlp * upstream).astype(LOW)
    gate_mlp_grad = jnp.sum(upstream * mlp_branch, axis=0)
    fc2_bias_part = jnp.sum(branch_grad, axis=0, dtype=FULL)
    fc2_weight_part = dot(activ, branch_grad, FIRST).astype(LOW)
    fc2_weight_part, branch_grad = lax.optimization_barrier((fc2_weight_part, branch_grad))
    fc2_weight_grad = reduce_weight(fc2_weight_part)
    activ_grad = dot(branch_grad, fc2_full, LAST)
    pre_grad = gelu_back(activ_grad)[0].astype(LOW)
    fc1_weight_part = dot(pre_grad, hidden_mlp, FIRST).astype(LOW)
    fc1_weight_part, pre_grad = lax.optimization_barrier((fc1_weight_part, pre_grad))
    fc1_weight_grad = reduce_weight(fc1_weight_part)
    fc1_bias_part = jnp.sum(pre_grad, axis=0, dtype=FULL)
    hidden_mlp_grad = dot(pre_grad, fc1_full)
    shift_mlp_grad = jnp.sum(hidden_mlp_grad, axis=0)
    scale_mlp_grad = jnp.sum(hidden_mlp_grad * normed_mlp, axis=0)
    mixed_grad = upstream + norm_back(normed_mlp, mlp_scale, hidden_mlp_grad * (1.0 + scale_mlp))
    gate_attn_grad = jnp.sum(mixed_grad * attn_branch, axis=0)
    attn_grad = (gate_attn * mixed_grad).astype(LOW)
    out_bias_part = jnp.sum(attn_grad, axis=0, dtype=FULL)
    out_weight_part = dot(attended, attn_grad, FIRST).astype(LOW)
    attended_grad = dot(attn_grad, out_full, LAST).astype(LOW)
    out_weight_part = out_weight_part.reshape(local, groups, HDIM, width)
    first_parts, projected_grad = [], []
    for chunk in range(local):
        if chunk:
            attended_grad = after(attended_grad, projected_grad[0], fc2_weight_grad)
        part_grad = attend_back(projected, attended_grad, groups, chunk)
        weight_part = dot(part_grad, hidden_attn, FIRST).astype(LOW)
        first_parts.append(weight_part.reshape(groups, three, width))
        first_parts.append(out_weight_part[chunk])
        projected_grad.append(part_grad)
    first_part = jnp.concatenate(first_parts, axis=1).reshape(-1, width)
    projected_grad = after(tuple(projected_grad), first_part, fc1_weight_grad)
    first_grad = reduce_weight(first_part).astype(FULL)
    first_grad = jnp.transpose(first_grad.reshape(local, 4, HDIM, width), (1, 0, 2, 3))
    first_grad = first_grad.reshape(4, local_width, width)
    qkv_weight_grad = jnp.transpose(first_grad[:3], (2, 0, 1))
    out_weight_grad = first_grad[3]
    fc1_weight_grad = fc1_weight_grad.astype(FULL).T
    fc2_weight_grad = fc2_weight_grad.astype(FULL)
    hidden_attn_grad = dot(jnp.concatenate(projected_grad, axis=1), qkv_full)
    qkv_bias_part = jnp.concatenate([jnp.sum(part, axis=0, dtype=FULL) for part in projected_grad])
    shift_attn_grad = jnp.sum(hidden_attn_grad, axis=0)
    scale_attn_grad = jnp.sum(hidden_attn_grad * normed_attn, axis=0)
    tokens_grad = mixed_grad + norm_back(
        normed_attn, attn_scale, hidden_attn_grad * (1.0 + scale_attn)
    )
    tokens_grad = from_slots(tokens_grad.astype(LOW), slots).astype(FULL)
    tokens_grad = jnp.transpose(tokens_grad, (1, 0, 2))

    mod_row = jnp.concatenate(
        [
            shift_attn_grad,
            scale_attn_grad,
            gate_attn_grad,
            shift_mlp_grad,
            scale_mlp_grad,
            gate_mlp_grad,
        ]
    ).astype(LOW)
    mod_mine = pair_gather(mod_row.reshape(groups, mod_width), "tensor")
    mod_mine = lax.dynamic_index_in_dim(mod_mine, here, 1, False)
    mod_grad = pair_gather(mod_mine, "dp").reshape(-1, mod_width)
    activated_all = pair_gather(jnp.pad(activated, ((start, groups - slots - start), (0, 0))), "dp")
    ada_weight_grad = dot(activated_all.reshape(-1, width), mod_grad, FIRST)
    ada_bias_grad = jnp.sum(mod_grad, axis=0, dtype=FULL)
    cond_sum = pair_sum(dot(mod_mine[start : start + slots], ada_weight, LAST), "tensor")
    condition_grad = silu_back(cond_sum)[0]
    bias_sum = jnp.concatenate([out_bias_part, fc2_bias_part, fc1_bias_part, qkv_bias_part])
    bias_sum = pair_sum(pair_sum(bias_sum, "tensor"), "dp")
    out_bias_grad, fc2_bias_grad = bias_sum[:width], bias_sum[width : 2 * width]
    fc1_bias_grad = lax.dynamic_slice_in_dim(bias_sum, 2 * width + here * hidden_local, hidden_local, 0)
    qkv_start = 2 * width + groups * hidden_local
    qkv_bias_sum = bias_sum[qkv_start:].reshape(local, groups, three)
    qkv_bias_sum = lax.dynamic_index_in_dim(qkv_bias_sum, here, 1, False).reshape(local, 3, HDIM)
    qkv_bias_sum = jnp.transpose(qkv_bias_sum, (1, 0, 2)).reshape(3, local_width)
    qkv_bias_grad = jnp.stack([qkv_bias_sum[0], qkv_bias_sum[2]])
    return (
        output,
        tokens_grad,
        condition_grad,
        ada_weight_grad,
        ada_bias_grad,
        qkv_weight_grad,
        qkv_bias_grad,
        out_weight_grad,
        out_bias_grad,
        fc1_weight_grad,
        fc1_bias_grad,
        fc2_weight_grad,
        fc2_bias_grad,
    )


def solution(mesh):
    return jax.shard_map(
        on_device,
        mesh=mesh,
        in_specs=(
            P("tensor", "dp", None),
            P("dp", None),
            P("dp"),
            P(None, "tensor"),
            P("tensor"),
            P(None, None, "tensor"),
            P(None, "tensor"),
            P("tensor", None),
            P(),
            P(None, "tensor"),
            P("tensor"),
            P("tensor", None),
            P(),
            P("tensor", "dp", None),
        ),
        out_specs=(
            P("tensor", "dp", None),
            P("tensor", "dp", None),
            P("dp", None),
            P(None, "tensor"),
            P("tensor"),
            P(None, None, "tensor"),
            P(None, "tensor"),
            P("tensor", None),
            P(),
            P(None, "tensor"),
            P("tensor"),
            P("tensor", None),
            P(),
        ),
        check_vma=False,
    )
```

```python
import functools

import jax
import jax.numpy as jnp
from jax import lax
from jax.experimental import pallas as pl
from jax.experimental.pallas import tpu as pltpu
from jax.sharding import PartitionSpec as P

HDIM = 72
LOW = jnp.bfloat16
FULL = jnp.float32
LAST = (((1,), (1,)), ((), ()))
FIRST = (((0,), (0,)), ((), ()))
PLAIN = (((1,), (0,)), ((), ()))
ROWS = 256
CORE = 1
SIDE = 2


def dot(left, right, dims=PLAIN):
    return lax.dot_general(left, right, dims, preferred_element_type=FULL)


def layer_norm(values):
    average = jnp.mean(values, axis=-1, keepdims=True)
    centred = values - average
    variance = jnp.mean(centred * centred, axis=-1, keepdims=True)
    scale = lax.rsqrt(variance + 1e-06)
    return centred * scale, scale


def norm_back(normed, scale, grad):
    first = jnp.mean(grad, axis=-1, keepdims=True)
    second = jnp.mean(grad * normed, axis=-1, keepdims=True)
    return (grad - first - normed * second) * scale


def gelu_tanh(values):
    return jax.nn.gelu(values, approximate=True)


def soft_rows(query_block, keys):
    scores = dot(query_block, keys, LAST)
    peak = jnp.max(scores, axis=-1, keepdims=True)
    raised = jnp.exp((scores - peak) * (HDIM**-0.5))
    return raised * (1.0 / jnp.sum(raised, axis=-1, keepdims=True))


def column(head, part):
    return (head * 3 + part) * HDIM


def attend_kernel(heads, base, projected, attended, queries, keys, values, results):
    seq = projected.shape[0]
    block = min(ROWS, seq)
    for head in range(heads):
        for part, held in enumerate((queries, keys, values)):
            at = base + column(head, part)
            held[head] = projected[:, at : at + HDIM]

    def one_head(head, carry):
        key_rows, value_rows = keys[head], values[head]
        for start in range(0, seq, block):
            soft = soft_rows(queries[head, start : start + block], key_rows)
            results[head, start : start + block] = dot(soft.astype(LOW), value_rows).astype(LOW)
        return carry

    lax.fori_loop(0, heads, one_head, 0)
    for head in range(heads):
        attended[:, head * HDIM : (head + 1) * HDIM] = results[head]


def attend(projected, heads, chunk):
    seq = projected.shape[0]
    held = pltpu.VMEM((heads, seq, HDIM), LOW)
    return pl.pallas_call(
        functools.partial(attend_kernel, heads, chunk * column(heads, 0)),
        out_shape=jax.ShapeDtypeStruct((seq, heads * HDIM), LOW),
        in_specs=[pl.BlockSpec(memory_space=pltpu.VMEM)],
        out_specs=pl.BlockSpec(memory_space=pltpu.VMEM),
        scratch_shapes=[held, held, held, held],
        compiler_params=pltpu.CompilerParams(vmem_limit_bytes=48 * 1024 * 1024),
        cost_estimate=pl.CostEstimate(
            flops=heads * seq * seq * 2048,
            bytes_accessed=8 * heads * HDIM * seq,
            transcendentals=heads * seq * seq,
        ),
    )(projected)


def attend_back_kernel(
    heads, base, projected, attended_grad, projected_grad, queries, keys, values, grads
):
    seq = projected.shape[0]
    block = min(ROWS, seq)
    score_scale = HDIM**-0.5
    first = base // 3
    for head in range(heads):
        for part, held in enumerate((queries, keys, values)):
            at = base + column(head, part)
            held[head] = projected[:, at : at + HDIM]
        at = first + head * HDIM
        grads[head] = attended_grad[:, at : at + HDIM]

    def one_head(head, carry):
        key_rows, value_rows = keys[head], values[head]
        key_total = value_total = None
        for start in range(0, seq, block):
            query_block = queries[head, start : start + block]
            grad_block = grads[head, start : start + block]
            soft = soft_rows(query_block, key_rows)
            soft_grad = dot(grad_block, value_rows, LAST)
            row_dot = jnp.sum(soft * soft_grad, axis=-1, keepdims=True)
            score_grad = (soft * (soft_grad - row_dot)).astype(LOW)
            queries[head, start : start + block] = (
                dot(score_grad, key_rows) * score_scale
            ).astype(LOW)
            key_part = dot(query_block, score_grad, FIRST)
            value_part = dot(grad_block, soft.astype(LOW), FIRST)
            key_total = key_part if key_total is None else key_total + key_part
            value_total = value_part if value_total is None else value_total + value_part
        keys[head] = (key_total * score_scale).T.astype(LOW)
        values[head] = value_total.T.astype(LOW)
        return carry

    lax.fori_loop(0, heads, one_head, 0)
    for head in range(heads):
        for part, held in enumerate((queries, keys, values)):
            at = column(head, part)
            projected_grad[:, at : at + HDIM] = held[head]


def attend_back(projected, attended_grad, heads, chunk):
    seq = projected.shape[0]
    held = pltpu.VMEM((heads, seq, HDIM), LOW)
    whole = pl.BlockSpec(memory_space=pltpu.VMEM)
    return pl.pallas_call(
        functools.partial(attend_back_kernel, heads, chunk * column(heads, 0)),
        out_shape=jax.ShapeDtypeStruct((seq, column(heads, 0)), LOW),
        in_specs=[whole, whole],
        out_specs=whole,
        scratch_shapes=[held, held, held, held],
        compiler_params=pltpu.CompilerParams(vmem_limit_bytes=48 * 1024 * 1024),
        cost_estimate=pl.CostEstimate(
            flops=heads * seq * seq * 4096,
            bytes_accessed=14 * heads * HDIM * seq,
            transcendentals=heads * seq * seq,
        ),
    )(projected, attended_grad)


def low(values):
    return lax.optimization_barrier(values.astype(LOW))


def add(*terms):
    total = terms[0].astype(FULL)
    for term in terms[1:]:
        total = total + term.astype(FULL)
    return total


def partner(values, axis, bit):
    return lax.ppermute(values, axis, [(i, i ^ bit) for i in range(lax.axis_size(axis))])


def bits_of(axis, start=1):
    found, bit = [], start
    while bit < lax.axis_size(axis):
        found.append(bit)
        bit *= 2
    return found


def order_by(flag, one, two, axis):
    return jnp.concatenate([jnp.where(flag, two, one), jnp.where(flag, one, two)], axis=axis)


def pair_sum(values, axis, start=1):
    for bit in bits_of(axis, start):
        values = values + partner(values, axis, bit)
    return values


def pair_gather(values, axis):
    here = lax.axis_index(axis)
    held = values[None]
    for bit in bits_of(axis):
        held = order_by((here & bit) != 0, held, partner(held, axis, bit), 0)
    return held


def after(value, *others):
    return lax.optimization_barrier((value, *others))[0]


def gather_weight(shard):
    share = shard.shape[0] // lax.axis_size("dp")
    mine = lax.dynamic_slice_in_dim(shard, lax.axis_index("dp") * share, share, 0)
    return lax.all_gather(mine, ("tensor", "dp"), axis=0, tiled=True)


def halves(values, flag):
    size = values.shape[1] // 2
    return (
        lax.dynamic_slice_in_dim(values, flag * size, size, 1),
        lax.dynamic_slice_in_dim(values, (1 - flag) * size, size, 1),
    )


def pair_reduce(terms, bit):
    keep, send = halves(terms, (lax.axis_index("dp") & bit) // bit)
    return add(keep, partner(send, "dp", bit)).astype(LOW)


def scatter(terms):
    held = terms.reshape(-1, terms.shape[2])
    return lax.psum_scatter(held, "tensor", scatter_dimension=0, tiled=True)


def spread(held):
    for bit in bits_of("dp", 4):
        held = low(add(held, partner(held, "dp", bit)))
    for bit in (SIDE, CORE):
        held = order_by((lax.axis_index("dp") & bit) != 0, held, partner(held, "dp", bit), 0)
    return held


def slot_start(slots):
    return (lax.axis_size("tensor") - slots) // 2


def to_slots(pieces):
    slots, rows, width = pieces.shape
    groups, here = lax.axis_size("tensor"), lax.axis_index("tensor")
    start = slot_start(slots)
    parts = []
    for step in range(groups):
        slot = jnp.clip(lax.rem(here + step, groups) - start, 0, slots - 1)
        piece = lax.dynamic_index_in_dim(pieces, slot, 0, False)
        if step:
            pairs = [(i, (i + step) % groups) for i in range(groups)]
            pairs = [pair for pair in pairs if start <= pair[1] < start + slots]
            piece = lax.ppermute(piece, "tensor", pairs)
        parts.append(piece)
    return jnp.concatenate(parts, axis=0)


def send_back(values, slots, steps):
    groups = lax.axis_size("tensor")
    start = slot_start(slots)
    rows = values.shape[0] // groups
    parts = []
    for step in steps:
        piece = values[step * rows : (step + 1) * rows]
        if step:
            pairs = [((i + step) % groups, i) for i in range(groups)]
            pairs = [pair for pair in pairs if start <= pair[0] < start + slots]
            piece = lax.ppermute(piece, "tensor", pairs)
        parts.append(piece)
    return parts


def from_slots(parts, slots):
    groups, here = lax.axis_size("tensor"), lax.axis_index("tensor")
    start = slot_start(slots)
    twice = jnp.stack(parts + parts, axis=0)
    return lax.dynamic_slice_in_dim(twice, lax.rem(groups + start - here, groups), slots, 0)


def on_device(
    tokens,
    condition,
    counts,
    ada_weight,
    ada_bias,
    qkv_weight,
    qkv_bias,
    out_weight,
    out_bias,
    fc1_weight,
    fc1_bias,
    fc2_weight,
    fc2_bias,
    out_grad,
):
    local_rows, slots, width = tokens.shape
    groups, here = lax.axis_size("tensor"), lax.axis_index("tensor")
    assert slots <= groups
    seq = local_rows * groups
    local_width = qkv_weight.shape[2]
    local = local_width // HDIM
    three = 3 * HDIM
    unit = 4 * HDIM
    start = slot_start(slots)
    hidden_local = fc1_weight.shape[1]
    live = ((here >= start) & (here - start < counts[0])).astype(FULL)

    qkv_rows = jnp.transpose(qkv_weight, (1, 2, 0)).reshape(3, local, HDIM, width)
    out_rows = out_weight.reshape(1, local, HDIM, width)
    first = jnp.transpose(jnp.concatenate([qkv_rows, out_rows]), (1, 0, 2, 3))
    first = gather_weight(first.reshape(local * unit, width)).reshape(groups, local, unit, width)
    fc1_full = gather_weight(fc1_weight.T)
    fc2_full = gather_weight(fc2_weight)
    first = jnp.transpose(first, (1, 0, 2, 3))
    qkv_full = first[:, :, :three].reshape(-1, width)
    out_full = first[:, :, three:].reshape(-1, width)

    silu_value, silu_back = jax.vjp(jax.nn.silu, condition.astype(FULL))
    activated = silu_value.astype(LOW)
    mod_local = dot(activated, ada_weight) + ada_bias.astype(FULL)
    mod_width = mod_local.shape[1]
    qkv_three = jnp.stack([qkv_bias[0], jnp.zeros_like(qkv_bias[0]), qkv_bias[1]])
    qkv_three = jnp.transpose(qkv_three.reshape(3, local, HDIM), (1, 0, 2)).reshape(-1).astype(FULL)
    small = jnp.concatenate([mod_local.reshape(-1), qkv_three, fc1_bias.astype(FULL)])
    small = pair_gather(small, "tensor")
    slot = jnp.clip(here - start, 0, slots - 1)
    modulation = small[:, : slots * mod_width].reshape(groups, slots, mod_width)
    modulation = lax.dynamic_index_in_dim(modulation, slot, 1, False).reshape(6, 1, width)
    shift_attn, scale_attn, gate_attn, shift_mlp, scale_mlp, gate_mlp = modulation
    qkv_bias_full = small[:, slots * mod_width : slots * mod_width + local * three]
    qkv_bias_full = jnp.transpose(qkv_bias_full.reshape(groups, local, three), (1, 0, 2)).reshape(-1)
    fc1_bias_full = small[:, slots * mod_width + local * three :].reshape(-1)

    inputs = to_slots(jnp.transpose(tokens, (1, 0, 2))).astype(FULL)
    normed_attn, attn_scale = layer_norm(inputs)
    hidden_attn = (normed_attn * (1.0 + scale_attn) + shift_attn).astype(LOW)
    projected = (dot(hidden_attn, qkv_full, LAST) + qkv_bias_full).astype(LOW)
    attended = [attend(projected, groups, chunk) for chunk in range(local)]
    attended = jnp.concatenate(attended, axis=1)
    attn_branch = dot(attended, out_full) + out_bias.astype(FULL)
    mixed = inputs + gate_attn * attn_branch
    normed_mlp, mlp_scale = layer_norm(mixed)
    hidden_mlp = (normed_mlp * (1.0 + scale_mlp) + shift_mlp).astype(LOW)
    pre_act = dot(hidden_mlp, fc1_full, LAST) + fc1_bias_full
    activ_value, gelu_back = jax.vjp(gelu_tanh, pre_act)
    activ = activ_value.astype(LOW)
    mlp_branch = dot(activ, fc2_full) + fc2_bias.astype(FULL)
    output = (live * (mixed + gate_mlp * mlp_branch)).astype(LOW)

    out_grad, _ = lax.optimization_barrier((out_grad, projected))
    upstream = live * to_slots(jnp.transpose(out_grad, (1, 0, 2))).astype(FULL)
    branch_grad = (gate_mlp * upstream).astype(LOW)
    gate_mlp_grad = jnp.sum(upstream * mlp_branch, axis=0)
    fc2_bias_part = jnp.sum(branch_grad, axis=0, dtype=FULL)
    fc2_part = dot(activ, branch_grad, FIRST).astype(LOW)
    fc2_part = pair_reduce(fc2_part.reshape(groups, hidden_local, width), CORE)
    branch_grad = after(branch_grad, fc2_part)
    fc2_part = pair_reduce(fc2_part, SIDE)
    activ_grad = dot(branch_grad, fc2_full, LAST)
    pre_grad = gelu_back(activ_grad)[0].astype(LOW)
    fc1_part = dot(pre_grad, hidden_mlp, FIRST).astype(LOW)
    pre_grad = after(pre_grad, fc1_part, fc2_part)
    fc2_part = scatter(fc2_part)
    fc1_part = pair_reduce(fc1_part.reshape(groups, hidden_local, width), CORE)
    fc1_bias_part = jnp.sum(pre_grad, axis=0, dtype=FULL)
    hidden_mlp_grad = dot(pre_grad, fc1_full)
    shift_mlp_grad = jnp.sum(hidden_mlp_grad, axis=0)
    scale_mlp_grad = jnp.sum(hidden_mlp_grad * normed_mlp, axis=0)
    mixed_grad = upstream + norm_back(normed_mlp, mlp_scale, hidden_mlp_grad * (1.0 + scale_mlp))
    gate_attn_grad = jnp.sum(mixed_grad * attn_branch, axis=0)
    attn_grad = (gate_attn * mixed_grad).astype(LOW)
    out_bias_part = jnp.sum(attn_grad, axis=0, dtype=FULL)
    out_weight_part = dot(attended, attn_grad, FIRST).astype(LOW)
    attended_grad = dot(attn_grad, out_full, LAST).astype(LOW)
    out_weight_part = out_weight_part.reshape(local, groups, HDIM, width)
    attended_grad = after(attended_grad, fc1_part, fc2_part)
    fc1_part = pair_reduce(fc1_part, SIDE)
    output = after(output, attended_grad)
    early = send_back(output, slots, range(groups // 2))
    first_parts, projected_grad = [], []
    for chunk in range(local):
        part_grad = attend_back(projected, attended_grad, groups, chunk)
        weight_part = dot(part_grad, hidden_attn, FIRST).astype(LOW)
        weight_part = weight_part.reshape(groups, three, width)
        part = pair_reduce(jnp.concatenate([weight_part, out_weight_part[chunk]], axis=1), CORE)
        projected_grad.append(part_grad)
        if not chunk:
            attended_grad = after(attended_grad, part, fc1_part, *early)
            fc1_part = scatter(fc1_part)
            output = after(output, attended_grad)
            late = send_back(output, slots, range(groups // 2, groups))
        else:
            projected_grad = after(projected_grad, part)
        first_parts.append(pair_reduce(part, SIDE))
    output = jnp.transpose(from_slots(early + late, slots), (1, 0, 2))
    first_part = scatter(jnp.concatenate(first_parts, axis=1))
    fc2_weight_grad = spread(fc2_part).astype(FULL)
    fc1_weight_grad = spread(fc1_part).astype(FULL).T
    first_grad = spread(first_part).reshape(4, local, -1, width)
    first_grad = jnp.transpose(first_grad, (1, 0, 2, 3)).astype(FULL)
    first_grad = jnp.transpose(first_grad.reshape(local, 4, HDIM, width), (1, 0, 2, 3))
    first_grad = first_grad.reshape(4, local_width, width)
    qkv_weight_grad = jnp.transpose(first_grad[:3], (2, 0, 1))
    out_weight_grad = first_grad[3]
    hidden_attn_grad = dot(jnp.concatenate(projected_grad, axis=1), qkv_full)
    qkv_bias_part = jnp.concatenate([jnp.sum(part, axis=0, dtype=FULL) for part in projected_grad])
    shift_attn_grad = jnp.sum(hidden_attn_grad, axis=0)
    scale_attn_grad = jnp.sum(hidden_attn_grad * normed_attn, axis=0)
    tokens_grad = mixed_grad + norm_back(
        normed_attn, attn_scale, hidden_attn_grad * (1.0 + scale_attn)
    )
    tokens_grad = after(tokens_grad.astype(LOW), fc1_part, *late)
    cut = groups - 2
    early = send_back(tokens_grad, slots, range(cut))
    tokens_grad = after(tokens_grad, first_part)
    late = send_back(tokens_grad, slots, range(cut, groups))
    tokens_grad = from_slots(early + late, slots).astype(FULL)
    tokens_grad = jnp.transpose(tokens_grad, (1, 0, 2))

    mod_row = jnp.concatenate(
        [
            shift_attn_grad,
            scale_attn_grad,
            gate_attn_grad,
            shift_mlp_grad,
            scale_mlp_grad,
            gate_mlp_grad,
        ]
    ).astype(LOW)
    mod_mine = pair_gather(mod_row.reshape(groups, mod_width), "tensor")
    mod_mine = lax.dynamic_index_in_dim(mod_mine, here, 1, False)
    mod_grad = pair_gather(mod_mine, "dp").reshape(-1, mod_width)
    activated_all = pair_gather(jnp.pad(activated, ((start, groups - slots - start), (0, 0))), "dp")
    ada_weight_grad = dot(activated_all.reshape(-1, width), mod_grad, FIRST)
    ada_bias_grad = jnp.sum(mod_grad, axis=0, dtype=FULL)
    cond_sum = pair_sum(dot(mod_mine[start : start + slots], ada_weight, LAST), "tensor")
    condition_grad = silu_back(cond_sum)[0]
    bias_sum = jnp.concatenate([out_bias_part, fc2_bias_part, fc1_bias_part, qkv_bias_part])
    bias_sum = pair_sum(pair_sum(bias_sum, "tensor"), "dp")
    out_bias_grad, fc2_bias_grad = bias_sum[:width], bias_sum[width : 2 * width]
    fc1_bias_grad = lax.dynamic_slice_in_dim(bias_sum, 2 * width + here * hidden_local, hidden_local, 0)
    qkv_start = 2 * width + groups * hidden_local
    qkv_bias_sum = bias_sum[qkv_start:].reshape(local, groups, three)
    qkv_bias_sum = lax.dynamic_index_in_dim(qkv_bias_sum, here, 1, False).reshape(local, 3, HDIM)
    qkv_bias_sum = jnp.transpose(qkv_bias_sum, (1, 0, 2)).reshape(3, local_width)
    qkv_bias_grad = jnp.stack([qkv_bias_sum[0], qkv_bias_sum[2]])
    return (
        output,
        tokens_grad,
        condition_grad,
        ada_weight_grad,
        ada_bias_grad,
        qkv_weight_grad,
        qkv_bias_grad,
        out_weight_grad,
        out_bias_grad,
        fc1_weight_grad,
        fc1_bias_grad,
        fc2_weight_grad,
        fc2_bias_grad,
    )


def solution(mesh):
    return jax.shard_map(
        on_device,
        mesh=mesh,
        in_specs=(
            P("tensor", "dp", None),
            P("dp", None),
            P("dp"),
            P(None, "tensor"),
            P("tensor"),
            P(None, None, "tensor"),
            P(None, "tensor"),
            P("tensor", None),
            P(),
            P(None, "tensor"),
            P("tensor"),
            P("tensor", None),
            P(),
            P("tensor", "dp", None),
        ),
        out_specs=(
            P("tensor", "dp", None),
            P("tensor", "dp", None),
            P("dp", None),
            P(None, "tensor"),
            P("tensor"),
            P(None, None, "tensor"),
            P(None, "tensor"),
            P("tensor", None),
            P(),
            P(None, "tensor"),
            P("tensor"),
            P("tensor", None),
            P(),
        ),
        check_vma=False,
    )
```

```python
import functools

import jax
import jax.numpy as jnp
from jax import lax
from jax.experimental import pallas as pl
from jax.experimental.pallas import tpu as pltpu
from jax.sharding import PartitionSpec as P

HDIM = 72
LOW = jnp.bfloat16
FULL = jnp.float32
LAST = (((1,), (1,)), ((), ()))
FIRST = (((0,), (0,)), ((), ()))
PLAIN = (((1,), (0,)), ((), ()))
ROWS = 256
CORE = 1
SIDE = 2


def dot(left, right, dims=PLAIN):
    return lax.dot_general(left, right, dims, preferred_element_type=FULL)


def layer_norm(values):
    average = jnp.mean(values, axis=-1, keepdims=True)
    centred = values - average
    variance = jnp.mean(centred * centred, axis=-1, keepdims=True)
    scale = lax.rsqrt(variance + 1e-06)
    return centred * scale, scale


def norm_back(normed, scale, grad):
    first = jnp.mean(grad, axis=-1, keepdims=True)
    second = jnp.mean(grad * normed, axis=-1, keepdims=True)
    return (grad - first - normed * second) * scale


def gelu_tanh(values):
    return jax.nn.gelu(values, approximate=True)


def soft_rows(query_block, keys):
    scores = dot(query_block, keys, LAST)
    peak = jnp.max(scores, axis=-1, keepdims=True)
    raised = jnp.exp((scores - peak) * (HDIM**-0.5))
    return raised * (1.0 / jnp.sum(raised, axis=-1, keepdims=True))


def column(head, part):
    return (head * 3 + part) * HDIM


def attend_kernel(heads, base, projected, attended, queries, keys, values, results):
    seq = projected.shape[0]
    block = min(ROWS, seq)
    for head in range(heads):
        for part, held in enumerate((queries, keys, values)):
            at = base + column(head, part)
            held[head] = projected[:, at : at + HDIM]

    def one_head(head, carry):
        key_rows, value_rows = keys[head], values[head]
        for start in range(0, seq, block):
            soft = soft_rows(queries[head, start : start + block], key_rows)
            results[head, start : start + block] = dot(soft.astype(LOW), value_rows).astype(LOW)
        return carry

    lax.fori_loop(0, heads, one_head, 0)
    for head in range(heads):
        attended[:, head * HDIM : (head + 1) * HDIM] = results[head]


def attend(projected, heads, chunk):
    seq = projected.shape[0]
    held = pltpu.VMEM((heads, seq, HDIM), LOW)
    return pl.pallas_call(
        functools.partial(attend_kernel, heads, chunk * column(heads, 0)),
        out_shape=jax.ShapeDtypeStruct((seq, heads * HDIM), LOW),
        in_specs=[pl.BlockSpec(memory_space=pltpu.VMEM)],
        out_specs=pl.BlockSpec(memory_space=pltpu.VMEM),
        scratch_shapes=[held, held, held, held],
        compiler_params=pltpu.CompilerParams(vmem_limit_bytes=48 * 1024 * 1024),
        cost_estimate=pl.CostEstimate(
            flops=heads * seq * seq * 2048,
            bytes_accessed=8 * heads * HDIM * seq,
            transcendentals=heads * seq * seq,
        ),
    )(projected)


def attend_back_kernel(
    heads, base, projected, attended_grad, projected_grad, queries, keys, values, grads
):
    seq = projected.shape[0]
    block = min(ROWS, seq)
    score_scale = HDIM**-0.5
    first = base // 3
    for head in range(heads):
        for part, held in enumerate((queries, keys, values)):
            at = base + column(head, part)
            held[head] = projected[:, at : at + HDIM]
        at = first + head * HDIM
        grads[head] = attended_grad[:, at : at + HDIM]

    def one_head(head, carry):
        key_rows, value_rows = keys[head], values[head]
        key_total = value_total = None
        for start in range(0, seq, block):
            query_block = queries[head, start : start + block]
            grad_block = grads[head, start : start + block]
            soft = soft_rows(query_block, key_rows)
            soft_grad = dot(grad_block, value_rows, LAST)
            row_dot = jnp.sum(soft * soft_grad, axis=-1, keepdims=True)
            score_grad = (soft * (soft_grad - row_dot)).astype(LOW)
            queries[head, start : start + block] = (
                dot(score_grad, key_rows) * score_scale
            ).astype(LOW)
            key_part = dot(query_block, score_grad, FIRST)
            value_part = dot(grad_block, soft.astype(LOW), FIRST)
            key_total = key_part if key_total is None else key_total + key_part
            value_total = value_part if value_total is None else value_total + value_part
        keys[head] = (key_total * score_scale).T.astype(LOW)
        values[head] = value_total.T.astype(LOW)
        return carry

    lax.fori_loop(0, heads, one_head, 0)
    for head in range(heads):
        for part, held in enumerate((queries, keys, values)):
            at = column(head, part)
            projected_grad[:, at : at + HDIM] = held[head]


def attend_back(projected, attended_grad, heads, chunk):
    seq = projected.shape[0]
    held = pltpu.VMEM((heads, seq, HDIM), LOW)
    whole = pl.BlockSpec(memory_space=pltpu.VMEM)
    return pl.pallas_call(
        functools.partial(attend_back_kernel, heads, chunk * column(heads, 0)),
        out_shape=jax.ShapeDtypeStruct((seq, column(heads, 0)), LOW),
        in_specs=[whole, whole],
        out_specs=whole,
        scratch_shapes=[held, held, held, held],
        compiler_params=pltpu.CompilerParams(vmem_limit_bytes=48 * 1024 * 1024),
        cost_estimate=pl.CostEstimate(
            flops=heads * seq * seq * 4096,
            bytes_accessed=14 * heads * HDIM * seq,
            transcendentals=heads * seq * seq,
        ),
    )(projected, attended_grad)


def low(values):
    return lax.optimization_barrier(values.astype(LOW))


def add(*terms):
    total = terms[0].astype(FULL)
    for term in terms[1:]:
        total = total + term.astype(FULL)
    return total


def partner(values, axis, bit):
    return lax.ppermute(values, axis, [(i, i ^ bit) for i in range(lax.axis_size(axis))])


def bits_of(axis, start=1):
    found, bit = [], start
    while bit < lax.axis_size(axis):
        found.append(bit)
        bit *= 2
    return found


def order_by(flag, one, two, axis):
    return jnp.concatenate([jnp.where(flag, two, one), jnp.where(flag, one, two)], axis=axis)


def pair_sum(values, axis, start=1):
    for bit in bits_of(axis, start):
        values = values + partner(values, axis, bit)
    return values


def pair_gather(values, axis):
    here = lax.axis_index(axis)
    held = values[None]
    for bit in bits_of(axis):
        held = order_by((here & bit) != 0, held, partner(held, axis, bit), 0)
    return held


def after(value, *others):
    return lax.optimization_barrier((value, *others))[0]


def gather_weight(shard):
    share = shard.shape[0] // lax.axis_size("dp")
    mine = lax.dynamic_slice_in_dim(shard, lax.axis_index("dp") * share, share, 0)
    return lax.all_gather(mine, ("tensor", "dp"), axis=0, tiled=True)


def halves(values, flag):
    size = values.shape[1] // 2
    return (
        lax.dynamic_slice_in_dim(values, flag * size, size, 1),
        lax.dynamic_slice_in_dim(values, (1 - flag) * size, size, 1),
    )


def pair_reduce(terms, bit):
    keep, send = halves(terms, (lax.axis_index("dp") & bit) // bit)
    return add(keep, partner(send, "dp", bit)).astype(LOW)


def scatter(terms):
    held = terms.reshape(-1, terms.shape[2])
    return lax.psum_scatter(held, "tensor", scatter_dimension=0, tiled=True)


def spread(held):
    for bit in bits_of("dp", 4):
        held = low(add(held, partner(held, "dp", bit)))
    for bit in (SIDE, CORE):
        held = order_by((lax.axis_index("dp") & bit) != 0, held, partner(held, "dp", bit), 0)
    return held


def slot_start(slots):
    return (lax.axis_size("tensor") - slots) // 2


def to_slots(pieces):
    slots, rows, width = pieces.shape
    groups, here = lax.axis_size("tensor"), lax.axis_index("tensor")
    start = slot_start(slots)
    parts = []
    for step in range(groups):
        slot = jnp.clip(lax.rem(here + step, groups) - start, 0, slots - 1)
        piece = lax.dynamic_index_in_dim(pieces, slot, 0, False)
        if step:
            pairs = [(i, (i + step) % groups) for i in range(groups)]
            pairs = [pair for pair in pairs if start <= pair[1] < start + slots]
            piece = lax.ppermute(piece, "tensor", pairs)
        parts.append(piece)
    return jnp.concatenate(parts, axis=0)


def send_back(values, slots, steps):
    groups = lax.axis_size("tensor")
    start = slot_start(slots)
    rows = values.shape[0] // groups
    parts = []
    for step in steps:
        piece = values[step * rows : (step + 1) * rows]
        if step:
            pairs = [((i + step) % groups, i) for i in range(groups)]
            pairs = [pair for pair in pairs if start <= pair[0] < start + slots]
            piece = lax.ppermute(piece, "tensor", pairs)
        parts.append(piece)
    return parts


def from_slots(parts, slots):
    groups, here = lax.axis_size("tensor"), lax.axis_index("tensor")
    start = slot_start(slots)
    twice = jnp.stack(parts + parts, axis=0)
    return lax.dynamic_slice_in_dim(twice, lax.rem(groups + start - here, groups), slots, 0)


def on_device(
    tokens,
    condition,
    counts,
    ada_weight,
    ada_bias,
    qkv_weight,
    qkv_bias,
    out_weight,
    out_bias,
    fc1_weight,
    fc1_bias,
    fc2_weight,
    fc2_bias,
    out_grad,
):
    local_rows, slots, width = tokens.shape
    groups, here = lax.axis_size("tensor"), lax.axis_index("tensor")
    assert slots <= groups
    seq = local_rows * groups
    local_width = qkv_weight.shape[2]
    local = local_width // HDIM
    three = 3 * HDIM
    unit = 4 * HDIM
    start = slot_start(slots)
    hidden_local = fc1_weight.shape[1]
    live = ((here >= start) & (here - start < counts[0])).astype(FULL)

    qkv_rows = jnp.transpose(qkv_weight, (1, 2, 0)).reshape(3, local, HDIM, width)
    out_rows = out_weight.reshape(1, local, HDIM, width)
    first = jnp.transpose(jnp.concatenate([qkv_rows, out_rows]), (1, 0, 2, 3))
    first = gather_weight(first.reshape(local * unit, width)).reshape(groups, local, unit, width)
    fc1_full = gather_weight(fc1_weight.T)
    fc2_full = gather_weight(fc2_weight)
    first = jnp.transpose(first, (1, 0, 2, 3))
    qkv_full = first[:, :, :three].reshape(-1, width)
    out_full = first[:, :, three:].reshape(-1, width)

    silu_value, silu_back = jax.vjp(jax.nn.silu, condition.astype(FULL))
    activated = silu_value.astype(LOW)
    mod_local = dot(activated, ada_weight) + ada_bias.astype(FULL)
    mod_width = mod_local.shape[1]
    qkv_three = jnp.stack([qkv_bias[0], jnp.zeros_like(qkv_bias[0]), qkv_bias[1]])
    qkv_three = jnp.transpose(qkv_three.reshape(3, local, HDIM), (1, 0, 2)).reshape(-1).astype(FULL)
    small = jnp.concatenate([mod_local.reshape(-1), qkv_three, fc1_bias.astype(FULL)])
    small = pair_gather(small, "tensor")
    slot = jnp.clip(here - start, 0, slots - 1)
    modulation = small[:, : slots * mod_width].reshape(groups, slots, mod_width)
    modulation = lax.dynamic_index_in_dim(modulation, slot, 1, False).reshape(6, 1, width)
    shift_attn, scale_attn, gate_attn, shift_mlp, scale_mlp, gate_mlp = modulation
    qkv_bias_full = small[:, slots * mod_width : slots * mod_width + local * three]
    qkv_bias_full = jnp.transpose(qkv_bias_full.reshape(groups, local, three), (1, 0, 2)).reshape(-1)
    fc1_bias_full = small[:, slots * mod_width + local * three :].reshape(-1)

    inputs = to_slots(jnp.transpose(tokens, (1, 0, 2))).astype(FULL)
    normed_attn, attn_scale = layer_norm(inputs)
    hidden_attn = (normed_attn * (1.0 + scale_attn) + shift_attn).astype(LOW)
    projected = (dot(hidden_attn, qkv_full, LAST) + qkv_bias_full).astype(LOW)
    attended = [attend(projected, groups, chunk) for chunk in range(local)]
    attended = jnp.concatenate(attended, axis=1)
    attn_branch = dot(attended, out_full) + out_bias.astype(FULL)
    mixed = inputs + gate_attn * attn_branch
    normed_mlp, mlp_scale = layer_norm(mixed)
    hidden_mlp = (normed_mlp * (1.0 + scale_mlp) + shift_mlp).astype(LOW)
    pre_act = dot(hidden_mlp, fc1_full, LAST) + fc1_bias_full
    activ_value, gelu_back = jax.vjp(gelu_tanh, pre_act)
    activ = activ_value.astype(LOW)
    mlp_branch = dot(activ, fc2_full) + fc2_bias.astype(FULL)
    output = (live * (mixed + gate_mlp * mlp_branch)).astype(LOW)

    out_grad, _ = lax.optimization_barrier((out_grad, projected))
    upstream = live * to_slots(jnp.transpose(out_grad, (1, 0, 2))).astype(FULL)
    branch_grad = (gate_mlp * upstream).astype(LOW)
    gate_mlp_grad = jnp.sum(upstream * mlp_branch, axis=0)
    fc2_bias_part = jnp.sum(branch_grad, axis=0, dtype=FULL)
    fc2_part = dot(activ, branch_grad, FIRST).astype(LOW)
    fc2_part = pair_reduce(fc2_part.reshape(groups, hidden_local, width), CORE)
    branch_grad = after(branch_grad, fc2_part)
    fc2_part = pair_reduce(fc2_part, SIDE)
    activ_grad = dot(branch_grad, fc2_full, LAST)
    pre_grad = gelu_back(activ_grad)[0].astype(LOW)
    fc1_part = dot(pre_grad, hidden_mlp, FIRST).astype(LOW)
    pre_grad = after(pre_grad, fc1_part, fc2_part)
    fc2_part = scatter(fc2_part)
    fc1_part = pair_reduce(fc1_part.reshape(groups, hidden_local, width), CORE)
    fc1_bias_part = jnp.sum(pre_grad, axis=0, dtype=FULL)
    hidden_mlp_grad = dot(pre_grad, fc1_full)
    shift_mlp_grad = jnp.sum(hidden_mlp_grad, axis=0)
    scale_mlp_grad = jnp.sum(hidden_mlp_grad * normed_mlp, axis=0)
    mixed_grad = upstream + norm_back(normed_mlp, mlp_scale, hidden_mlp_grad * (1.0 + scale_mlp))
    gate_attn_grad = jnp.sum(mixed_grad * attn_branch, axis=0)
    attn_grad = (gate_attn * mixed_grad).astype(LOW)
    out_bias_part = jnp.sum(attn_grad, axis=0, dtype=FULL)
    out_weight_part = dot(attended, attn_grad, FIRST).astype(LOW)
    attended_grad = dot(attn_grad, out_full, LAST).astype(LOW)
    out_weight_part = out_weight_part.reshape(local, groups, HDIM, width)
    attended_grad = after(attended_grad, fc1_part, fc2_part)
    fc1_part = pair_reduce(fc1_part, SIDE)
    output = after(output, attended_grad)
    early = send_back(output, slots, range(groups // 2))
    first_parts, projected_grad = [], []
    for chunk in range(local):
        part_grad = attend_back(projected, attended_grad, groups, chunk)
        weight_part = dot(part_grad, hidden_attn, FIRST).astype(LOW)
        weight_part = weight_part.reshape(groups, three, width)
        part = pair_reduce(jnp.concatenate([weight_part, out_weight_part[chunk]], axis=1), CORE)
        projected_grad.append(part_grad)
        if not chunk:
            attended_grad = after(attended_grad, part, fc1_part, *early)
            fc1_part = scatter(fc1_part)
        else:
            projected_grad = after(projected_grad, part)
        first_parts.append(pair_reduce(part, SIDE))
    first_part = scatter(jnp.concatenate(first_parts, axis=1))
    fc2_weight_grad = spread(fc2_part).astype(FULL)
    fc1_weight_grad = spread(fc1_part).astype(FULL).T
    first_grad = spread(first_part).reshape(4, local, -1, width)
    first_grad = jnp.transpose(first_grad, (1, 0, 2, 3)).astype(FULL)
    first_grad = jnp.transpose(first_grad.reshape(local, 4, HDIM, width), (1, 0, 2, 3))
    first_grad = first_grad.reshape(4, local_width, width)
    qkv_weight_grad = jnp.transpose(first_grad[:3], (2, 0, 1))
    out_weight_grad = first_grad[3]
    hidden_attn_grad = dot(jnp.concatenate(projected_grad, axis=1), qkv_full)
    hidden_attn_grad = after(hidden_attn_grad, *first_parts)
    qkv_bias_part = jnp.concatenate([jnp.sum(part, axis=0, dtype=FULL) for part in projected_grad])
    shift_attn_grad = jnp.sum(hidden_attn_grad, axis=0)
    scale_attn_grad = jnp.sum(hidden_attn_grad * normed_attn, axis=0)
    tokens_grad = mixed_grad + norm_back(
        normed_attn, attn_scale, hidden_attn_grad * (1.0 + scale_attn)
    )
    tokens_grad = after(tokens_grad.astype(LOW), fc1_part)
    tokens_parts = send_back(tokens_grad, slots, range(groups // 2))
    both = jnp.concatenate([tokens_grad, output], axis=1)
    late = send_back(both, slots, range(groups // 2, groups - 2))
    late += send_back(after(both, first_part), slots, range(groups - 2, groups))
    tokens_parts += [part[:, :width] for part in late]
    output_parts = early + [part[:, width:] for part in late]
    tokens_grad = from_slots(tokens_parts, slots).astype(FULL)
    output = jnp.transpose(from_slots(output_parts, slots), (1, 0, 2))
    tokens_grad = jnp.transpose(tokens_grad, (1, 0, 2))

    mod_row = jnp.concatenate(
        [
            shift_attn_grad,
            scale_attn_grad,
            gate_attn_grad,
            shift_mlp_grad,
            scale_mlp_grad,
            gate_mlp_grad,
        ]
    ).astype(LOW)
    mod_mine = pair_gather(mod_row.reshape(groups, mod_width), "tensor")
    mod_mine = lax.dynamic_index_in_dim(mod_mine, here, 1, False)
    mod_grad = pair_gather(mod_mine, "dp").reshape(-1, mod_width)
    activated_all = pair_gather(jnp.pad(activated, ((start, groups - slots - start), (0, 0))), "dp")
    ada_weight_grad = dot(activated_all.reshape(-1, width), mod_grad, FIRST)
    ada_bias_grad = jnp.sum(mod_grad, axis=0, dtype=FULL)
    cond_sum = pair_sum(dot(mod_mine[start : start + slots], ada_weight, LAST), "tensor")
    condition_grad = silu_back(cond_sum)[0]
    bias_sum = jnp.concatenate([out_bias_part, fc2_bias_part, fc1_bias_part, qkv_bias_part])
    bias_sum = pair_sum(pair_sum(bias_sum, "tensor"), "dp")
    out_bias_grad, fc2_bias_grad = bias_sum[:width], bias_sum[width : 2 * width]
    fc1_bias_grad = lax.dynamic_slice_in_dim(bias_sum, 2 * width + here * hidden_local, hidden_local, 0)
    qkv_start = 2 * width + groups * hidden_local
    qkv_bias_sum = bias_sum[qkv_start:].reshape(local, groups, three)
    qkv_bias_sum = lax.dynamic_index_in_dim(qkv_bias_sum, here, 1, False).reshape(local, 3, HDIM)
    qkv_bias_sum = jnp.transpose(qkv_bias_sum, (1, 0, 2)).reshape(3, local_width)
    qkv_bias_grad = jnp.stack([qkv_bias_sum[0], qkv_bias_sum[2]])
    return (
        output,
        tokens_grad,
        condition_grad,
        ada_weight_grad,
        ada_bias_grad,
        qkv_weight_grad,
        qkv_bias_grad,
        out_weight_grad,
        out_bias_grad,
        fc1_weight_grad,
        fc1_bias_grad,
        fc2_weight_grad,
        fc2_bias_grad,
    )


def solution(mesh):
    return jax.shard_map(
        on_device,
        mesh=mesh,
        in_specs=(
            P("tensor", "dp", None),
            P("dp", None),
            P("dp"),
            P(None, "tensor"),
            P("tensor"),
            P(None, None, "tensor"),
            P(None, "tensor"),
            P("tensor", None),
            P(),
            P(None, "tensor"),
            P("tensor"),
            P("tensor", None),
            P(),
            P("tensor", "dp", None),
        ),
        out_specs=(
            P("tensor", "dp", None),
            P("tensor", "dp", None),
            P("dp", None),
            P(None, "tensor"),
            P("tensor"),
            P(None, None, "tensor"),
            P(None, "tensor"),
            P("tensor", None),
            P(),
            P(None, "tensor"),
            P("tensor"),
            P("tensor", None),
            P(),
        ),
        check_vma=False,
    )
```

```python
import functools

import jax
import jax.numpy as jnp
from jax import lax
from jax.experimental import pallas as pl
from jax.experimental.pallas import tpu as pltpu
from jax.sharding import PartitionSpec as P

HDIM = 72
LOW = jnp.bfloat16
FULL = jnp.float32
LAST = (((1,), (1,)), ((), ()))
FIRST = (((0,), (0,)), ((), ()))
PLAIN = (((1,), (0,)), ((), ()))
ROWS = 256
CORE = 1
SIDE = 2


def dot(left, right, dims=PLAIN):
    return lax.dot_general(left, right, dims, preferred_element_type=FULL)


def layer_norm(values):
    average = jnp.mean(values, axis=-1, keepdims=True)
    centred = values - average
    variance = jnp.mean(centred * centred, axis=-1, keepdims=True)
    scale = lax.rsqrt(variance + 1e-06)
    return centred * scale, scale


def norm_back(normed, scale, grad):
    first = jnp.mean(grad, axis=-1, keepdims=True)
    second = jnp.mean(grad * normed, axis=-1, keepdims=True)
    return (grad - first - normed * second) * scale


def gelu_tanh(values):
    return jax.nn.gelu(values, approximate=True)


def soft_rows(query_block, keys):
    scores = dot(query_block, keys, LAST)
    peak = jnp.max(scores, axis=-1, keepdims=True)
    raised = jnp.exp((scores - peak) * (HDIM**-0.5))
    return raised * (1.0 / jnp.sum(raised, axis=-1, keepdims=True))


def column(head, part):
    return (head * 3 + part) * HDIM


def attend_kernel(heads, base, projected, attended, queries, keys, values, results):
    seq = projected.shape[0]
    block = min(ROWS, seq)
    for head in range(heads):
        for part, held in enumerate((queries, keys, values)):
            at = base + column(head, part)
            held[head] = projected[:, at : at + HDIM]

    def one_head(head, carry):
        key_rows, value_rows = keys[head], values[head]
        for start in range(0, seq, block):
            soft = soft_rows(queries[head, start : start + block], key_rows)
            results[head, start : start + block] = dot(soft.astype(LOW), value_rows).astype(LOW)
        return carry

    lax.fori_loop(0, heads, one_head, 0)
    for head in range(heads):
        attended[:, head * HDIM : (head + 1) * HDIM] = results[head]


def attend(projected, heads, chunk):
    seq = projected.shape[0]
    held = pltpu.VMEM((heads, seq, HDIM), LOW)
    return pl.pallas_call(
        functools.partial(attend_kernel, heads, chunk * column(heads, 0)),
        out_shape=jax.ShapeDtypeStruct((seq, heads * HDIM), LOW),
        in_specs=[pl.BlockSpec(memory_space=pltpu.VMEM)],
        out_specs=pl.BlockSpec(memory_space=pltpu.VMEM),
        scratch_shapes=[held, held, held, held],
        compiler_params=pltpu.CompilerParams(vmem_limit_bytes=48 * 1024 * 1024),
        cost_estimate=pl.CostEstimate(
            flops=heads * seq * seq * 2048,
            bytes_accessed=8 * heads * HDIM * seq,
            transcendentals=heads * seq * seq,
        ),
    )(projected)


def attend_back_kernel(
    heads, base, projected, attended_grad, projected_grad, queries, keys, values, grads
):
    seq = projected.shape[0]
    block = min(ROWS, seq)
    score_scale = HDIM**-0.5
    first = base // 3
    for head in range(heads):
        for part, held in enumerate((queries, keys, values)):
            at = base + column(head, part)
            held[head] = projected[:, at : at + HDIM]
        at = first + head * HDIM
        grads[head] = attended_grad[:, at : at + HDIM]

    def one_head(head, carry):
        key_rows, value_rows = keys[head], values[head]
        key_total = value_total = None
        for start in range(0, seq, block):
            query_block = queries[head, start : start + block]
            grad_block = grads[head, start : start + block]
            soft = soft_rows(query_block, key_rows)
            soft_grad = dot(grad_block, value_rows, LAST)
            row_dot = jnp.sum(soft * soft_grad, axis=-1, keepdims=True)
            score_grad = (soft * (soft_grad - row_dot)).astype(LOW)
            queries[head, start : start + block] = (
                dot(score_grad, key_rows) * score_scale
            ).astype(LOW)
            key_part = dot(query_block, score_grad, FIRST)
            value_part = dot(grad_block, soft.astype(LOW), FIRST)
            key_total = key_part if key_total is None else key_total + key_part
            value_total = value_part if value_total is None else value_total + value_part
        keys[head] = (key_total * score_scale).T.astype(LOW)
        values[head] = value_total.T.astype(LOW)
        return carry

    lax.fori_loop(0, heads, one_head, 0)
    for head in range(heads):
        for part, held in enumerate((queries, keys, values)):
            at = column(head, part)
            projected_grad[:, at : at + HDIM] = held[head]


def attend_back(projected, attended_grad, heads, chunk):
    seq = projected.shape[0]
    held = pltpu.VMEM((heads, seq, HDIM), LOW)
    whole = pl.BlockSpec(memory_space=pltpu.VMEM)
    return pl.pallas_call(
        functools.partial(attend_back_kernel, heads, chunk * column(heads, 0)),
        out_shape=jax.ShapeDtypeStruct((seq, column(heads, 0)), LOW),
        in_specs=[whole, whole],
        out_specs=whole,
        scratch_shapes=[held, held, held, held],
        compiler_params=pltpu.CompilerParams(vmem_limit_bytes=48 * 1024 * 1024),
        cost_estimate=pl.CostEstimate(
            flops=heads * seq * seq * 4096,
            bytes_accessed=14 * heads * HDIM * seq,
            transcendentals=heads * seq * seq,
        ),
    )(projected, attended_grad)


def low(values):
    return lax.optimization_barrier(values.astype(LOW))


def add(*terms):
    total = terms[0].astype(FULL)
    for term in terms[1:]:
        total = total + term.astype(FULL)
    return total


def partner(values, axis, bit):
    return lax.ppermute(values, axis, [(i, i ^ bit) for i in range(lax.axis_size(axis))])


def bits_of(axis, start=1):
    found, bit = [], start
    while bit < lax.axis_size(axis):
        found.append(bit)
        bit *= 2
    return found


def order_by(flag, one, two, axis):
    return jnp.concatenate([jnp.where(flag, two, one), jnp.where(flag, one, two)], axis=axis)


def pair_sum(values, axis, start=1):
    for bit in bits_of(axis, start):
        values = values + partner(values, axis, bit)
    return values


def pair_gather(values, axis):
    here = lax.axis_index(axis)
    held = values[None]
    for bit in bits_of(axis):
        held = order_by((here & bit) != 0, held, partner(held, axis, bit), 0)
    return held


def after(value, *others):
    return lax.optimization_barrier((value, *others))[0]


def gather_weight(shard):
    share = shard.shape[0] // lax.axis_size("dp")
    mine = lax.dynamic_slice_in_dim(shard, lax.axis_index("dp") * share, share, 0)
    return lax.all_gather(mine, ("tensor", "dp"), axis=0, tiled=True)


def halves(values, flag):
    size = values.shape[1] // 2
    return (
        lax.dynamic_slice_in_dim(values, flag * size, size, 1),
        lax.dynamic_slice_in_dim(values, (1 - flag) * size, size, 1),
    )


def pair_reduce(terms, bit):
    keep, send = halves(terms, (lax.axis_index("dp") & bit) // bit)
    return add(keep, partner(send, "dp", bit)).astype(LOW)


def scatter(terms):
    held = terms.reshape(-1, terms.shape[2])
    return lax.psum_scatter(held, "tensor", scatter_dimension=0, tiled=True)


def spread(held):
    for bit in bits_of("dp", 4):
        held = low(add(held, partner(held, "dp", bit)))
    for bit in (SIDE, CORE):
        held = order_by((lax.axis_index("dp") & bit) != 0, held, partner(held, "dp", bit), 0)
    return held


def slot_start(slots):
    return (lax.axis_size("tensor") - slots) // 2


def to_slots(pieces):
    slots, rows, width = pieces.shape
    groups, here = lax.axis_size("tensor"), lax.axis_index("tensor")
    start = slot_start(slots)
    parts = []
    for step in range(groups):
        slot = jnp.clip(lax.rem(here + step, groups) - start, 0, slots - 1)
        piece = lax.dynamic_index_in_dim(pieces, slot, 0, False)
        if step:
            pairs = [(i, (i + step) % groups) for i in range(groups)]
            pairs = [pair for pair in pairs if start <= pair[1] < start + slots]
            piece = lax.ppermute(piece, "tensor", pairs)
        parts.append(piece)
    return jnp.concatenate(parts, axis=0)


def send_back(values, slots, steps):
    groups = lax.axis_size("tensor")
    start = slot_start(slots)
    rows = values.shape[0] // groups
    parts = []
    for step in steps:
        piece = values[step * rows : (step + 1) * rows]
        if step:
            pairs = [((i + step) % groups, i) for i in range(groups)]
            pairs = [pair for pair in pairs if start <= pair[0] < start + slots]
            piece = lax.ppermute(piece, "tensor", pairs)
        parts.append(piece)
    return parts


def from_slots(parts, slots):
    groups, here = lax.axis_size("tensor"), lax.axis_index("tensor")
    start = slot_start(slots)
    twice = jnp.stack(parts + parts, axis=0)
    return lax.dynamic_slice_in_dim(twice, lax.rem(groups + start - here, groups), slots, 0)


def on_device(
    tokens,
    condition,
    counts,
    ada_weight,
    ada_bias,
    qkv_weight,
    qkv_bias,
    out_weight,
    out_bias,
    fc1_weight,
    fc1_bias,
    fc2_weight,
    fc2_bias,
    out_grad,
):
    local_rows, slots, width = tokens.shape
    groups, here = lax.axis_size("tensor"), lax.axis_index("tensor")
    assert slots <= groups
    seq = local_rows * groups
    local_width = qkv_weight.shape[2]
    local = local_width // HDIM
    three = 3 * HDIM
    unit = 4 * HDIM
    start = slot_start(slots)
    hidden_local = fc1_weight.shape[1]
    live = ((here >= start) & (here - start < counts[0])).astype(FULL)

    qkv_rows = jnp.transpose(qkv_weight, (1, 2, 0)).reshape(3, local, HDIM, width)
    out_rows = out_weight.reshape(1, local, HDIM, width)
    first = jnp.transpose(jnp.concatenate([qkv_rows, out_rows]), (1, 0, 2, 3))
    first = gather_weight(first.reshape(local * unit, width)).reshape(groups, local, unit, width)
    fc1_full = gather_weight(fc1_weight.T)
    fc2_full = gather_weight(fc2_weight)
    first = jnp.transpose(first, (1, 0, 2, 3))
    qkv_full = first[:, :, :three].reshape(-1, width)
    out_full = first[:, :, three:].reshape(-1, width)

    silu_value, silu_back = jax.vjp(jax.nn.silu, condition.astype(FULL))
    activated = silu_value.astype(LOW)
    mod_local = dot(activated, ada_weight) + ada_bias.astype(FULL)
    mod_width = mod_local.shape[1]
    qkv_three = jnp.stack([qkv_bias[0], jnp.zeros_like(qkv_bias[0]), qkv_bias[1]])
    qkv_three = jnp.transpose(qkv_three.reshape(3, local, HDIM), (1, 0, 2)).reshape(-1).astype(FULL)
    small = jnp.concatenate([mod_local.reshape(-1), qkv_three, fc1_bias.astype(FULL)])
    small = pair_gather(small, "tensor")
    slot = jnp.clip(here - start, 0, slots - 1)
    modulation = small[:, : slots * mod_width].reshape(groups, slots, mod_width)
    modulation = lax.dynamic_index_in_dim(modulation, slot, 1, False).reshape(6, 1, width)
    shift_attn, scale_attn, gate_attn, shift_mlp, scale_mlp, gate_mlp = modulation
    qkv_bias_full = small[:, slots * mod_width : slots * mod_width + local * three]
    qkv_bias_full = jnp.transpose(qkv_bias_full.reshape(groups, local, three), (1, 0, 2)).reshape(-1)
    fc1_bias_full = small[:, slots * mod_width + local * three :].reshape(-1)

    inputs = to_slots(jnp.transpose(tokens, (1, 0, 2))).astype(FULL)
    normed_attn, attn_scale = layer_norm(inputs)
    hidden_attn = (normed_attn * (1.0 + scale_attn) + shift_attn).astype(LOW)
    projected = (dot(hidden_attn, qkv_full, LAST) + qkv_bias_full).astype(LOW)
    attended = [attend(projected, groups, chunk) for chunk in range(local)]
    attended = jnp.concatenate(attended, axis=1)
    attn_branch = dot(attended, out_full) + out_bias.astype(FULL)
    mixed = inputs + gate_attn * attn_branch
    normed_mlp, mlp_scale = layer_norm(mixed)
    hidden_mlp = (normed_mlp * (1.0 + scale_mlp) + shift_mlp).astype(LOW)
    pre_act = dot(hidden_mlp, fc1_full, LAST) + fc1_bias_full
    activ_value, gelu_back = jax.vjp(gelu_tanh, pre_act)
    activ = activ_value.astype(LOW)
    mlp_branch = dot(activ, fc2_full) + fc2_bias.astype(FULL)
    output = (live * (mixed + gate_mlp * mlp_branch)).astype(LOW)

    out_grad, _ = lax.optimization_barrier((out_grad, projected))
    upstream = live * to_slots(jnp.transpose(out_grad, (1, 0, 2))).astype(FULL)
    branch_grad = (gate_mlp * upstream).astype(LOW)
    gate_mlp_grad = jnp.sum(upstream * mlp_branch, axis=0)
    fc2_bias_part = jnp.sum(branch_grad, axis=0, dtype=FULL)
    fc2_part = dot(activ, branch_grad, FIRST).astype(LOW)
    fc2_part = pair_reduce(fc2_part.reshape(groups, hidden_local, width), CORE)
    branch_grad = after(branch_grad, fc2_part)
    fc2_part = pair_reduce(fc2_part, SIDE)
    activ_grad = dot(branch_grad, fc2_full, LAST)
    pre_grad = gelu_back(activ_grad)[0].astype(LOW)
    fc1_part = dot(pre_grad, hidden_mlp, FIRST).astype(LOW)
    pre_grad = after(pre_grad, fc1_part, fc2_part)
    fc2_part = scatter(fc2_part)
    fc1_part = pair_reduce(fc1_part.reshape(groups, hidden_local, width), CORE)
    fc1_bias_part = jnp.sum(pre_grad, axis=0, dtype=FULL)
    hidden_mlp_grad = dot(pre_grad, fc1_full)
    shift_mlp_grad = jnp.sum(hidden_mlp_grad, axis=0)
    scale_mlp_grad = jnp.sum(hidden_mlp_grad * normed_mlp, axis=0)
    mixed_grad = upstream + norm_back(normed_mlp, mlp_scale, hidden_mlp_grad * (1.0 + scale_mlp))
    gate_attn_grad = jnp.sum(mixed_grad * attn_branch, axis=0)
    attn_grad = (gate_attn * mixed_grad).astype(LOW)
    out_bias_part = jnp.sum(attn_grad, axis=0, dtype=FULL)
    out_weight_part = dot(attended, attn_grad, FIRST).astype(LOW)
    attended_grad = dot(attn_grad, out_full, LAST).astype(LOW)
    out_weight_part = out_weight_part.reshape(local, groups, HDIM, width)
    attended_grad = after(attended_grad, fc1_part, fc2_part)
    fc1_part = pair_reduce(fc1_part, SIDE)
    output = after(output, attended_grad)
    early = send_back(output, slots, range(groups // 2))
    first_parts, projected_grad = [], []
    for chunk in range(local):
        part_grad = attend_back(projected, attended_grad, groups, chunk)
        weight_part = dot(part_grad, hidden_attn, FIRST).astype(LOW)
        weight_part = weight_part.reshape(groups, three, width)
        part = pair_reduce(jnp.concatenate([weight_part, out_weight_part[chunk]], axis=1), CORE)
        projected_grad.append(part_grad)
        if not chunk:
            attended_grad = after(attended_grad, part, fc1_part, *early)
            fc1_part = scatter(fc1_part)
            output = after(output, attended_grad)
            late = send_back(output, slots, range(groups // 2, groups))
        else:
            projected_grad = after(projected_grad, part)
        first_parts.append(pair_reduce(part, SIDE))
    output = jnp.transpose(from_slots(early + late, slots), (1, 0, 2))
    first_part = scatter(jnp.concatenate(first_parts, axis=1))
    fc2_weight_grad = spread(fc2_part).astype(FULL)
    fc1_weight_grad = spread(fc1_part).astype(FULL).T
    first_grad = spread(first_part).reshape(4, local, -1, width)
    first_grad = jnp.transpose(first_grad, (1, 0, 2, 3)).astype(FULL)
    first_grad = jnp.transpose(first_grad.reshape(local, 4, HDIM, width), (1, 0, 2, 3))
    first_grad = first_grad.reshape(4, local_width, width)
    qkv_weight_grad = jnp.transpose(first_grad[:3], (2, 0, 1))
    out_weight_grad = first_grad[3]
    hidden_attn_grad = dot(jnp.concatenate(projected_grad, axis=1), qkv_full)
    hidden_attn_grad = after(hidden_attn_grad, *first_parts)
    qkv_bias_part = jnp.concatenate([jnp.sum(part, axis=0, dtype=FULL) for part in projected_grad])
    shift_attn_grad = jnp.sum(hidden_attn_grad, axis=0)
    scale_attn_grad = jnp.sum(hidden_attn_grad * normed_attn, axis=0)
    tokens_grad = mixed_grad + norm_back(
        normed_attn, attn_scale, hidden_attn_grad * (1.0 + scale_attn)
    )
    tokens_grad = after(tokens_grad.astype(LOW), fc1_part, *late)
    cut = groups // 2
    early = send_back(tokens_grad, slots, range(cut))
    tokens_grad = after(tokens_grad, first_part)
    late = send_back(tokens_grad, slots, range(cut, groups))
    tokens_grad = from_slots(early + late, slots).astype(FULL)
    tokens_grad = jnp.transpose(tokens_grad, (1, 0, 2))

    mod_row = jnp.concatenate(
        [
            shift_attn_grad,
            scale_attn_grad,
            gate_attn_grad,
            shift_mlp_grad,
            scale_mlp_grad,
            gate_mlp_grad,
        ]
    ).astype(LOW)
    mod_row = after(mod_row, first_part)
    mod_mine = pair_gather(mod_row.reshape(groups, mod_width), "tensor")
    mod_mine = lax.dynamic_index_in_dim(mod_mine, here, 1, False)
    mod_grad = pair_gather(mod_mine, "dp").reshape(-1, mod_width)
    activated_all = pair_gather(jnp.pad(activated, ((start, groups - slots - start), (0, 0))), "dp")
    ada_weight_grad = dot(activated_all.reshape(-1, width), mod_grad, FIRST)
    ada_bias_grad = jnp.sum(mod_grad, axis=0, dtype=FULL)
    cond_sum = pair_sum(dot(mod_mine[start : start + slots], ada_weight, LAST), "tensor")
    condition_grad = silu_back(cond_sum)[0]
    bias_sum = jnp.concatenate([out_bias_part, fc2_bias_part, fc1_bias_part, qkv_bias_part])
    bias_sum = pair_sum(pair_sum(bias_sum, "tensor"), "dp")
    out_bias_grad, fc2_bias_grad = bias_sum[:width], bias_sum[width : 2 * width]
    fc1_bias_grad = lax.dynamic_slice_in_dim(bias_sum, 2 * width + here * hidden_local, hidden_local, 0)
    qkv_start = 2 * width + groups * hidden_local
    qkv_bias_sum = bias_sum[qkv_start:].reshape(local, groups, three)
    qkv_bias_sum = lax.dynamic_index_in_dim(qkv_bias_sum, here, 1, False).reshape(local, 3, HDIM)
    qkv_bias_sum = jnp.transpose(qkv_bias_sum, (1, 0, 2)).reshape(3, local_width)
    qkv_bias_grad = jnp.stack([qkv_bias_sum[0], qkv_bias_sum[2]])
    return (
        output,
        tokens_grad,
        condition_grad,
        ada_weight_grad,
        ada_bias_grad,
        qkv_weight_grad,
        qkv_bias_grad,
        out_weight_grad,
        out_bias_grad,
        fc1_weight_grad,
        fc1_bias_grad,
        fc2_weight_grad,
        fc2_bias_grad,
    )


def solution(mesh):
    return jax.shard_map(
        on_device,
        mesh=mesh,
        in_specs=(
            P("tensor", "dp", None),
            P("dp", None),
            P("dp"),
            P(None, "tensor"),
            P("tensor"),
            P(None, None, "tensor"),
            P(None, "tensor"),
            P("tensor", None),
            P(),
            P(None, "tensor"),
            P("tensor"),
            P("tensor", None),
            P(),
            P("tensor", "dp", None),
        ),
        out_specs=(
            P("tensor", "dp", None),
            P("tensor", "dp", None),
            P("dp", None),
            P(None, "tensor"),
            P("tensor"),
            P(None, None, "tensor"),
            P(None, "tensor"),
            P("tensor", None),
            P(),
            P(None, "tensor"),
            P("tensor"),
            P("tensor", None),
            P(),
        ),
        check_vma=False,
    )
```
